256 devices in a mesh: row: 32 (over x, y, core), col: 8 (over z).
Axes of the slice: x: 4, y: 4, z: 8, core: 2. Of those that a mesh axis runs over, the one named last changes fastest.
Arguments:
- patches: bfloat16 [16, 256, 6144], P(None, 'col', 'row'), may hold values from -30 to 30
- out_grads: bfloat16 [16, 256, 24576], P(None, 'row', 'col'), may hold values from -8 to 8
Outputs:
- clipped: float32 [6144, 24576], P('row', 'col')
- norms: float32 [16], replicated
The draws below stay inside these ranges and needn't reach their ends.
All inputs are finite; a program needn't handle non-finite values.
Results may differ from the reference program's by a relative error of at most 0.0003.
Values may be sent and summed in bfloat16 or wider, within the bound.
A program may use at most 128 MiB of HBM per device.

```python
import math
import jax
import jax.numpy as jnp
from jax import lax

D = 6144
HID = 24576
SEQ = 256
IMAGES = 16


def log_scales(key, shape, low, high):
    value = jnp.exp(jax.random.uniform(key, shape, jnp.float32, math.log(low), math.log(high)))
    return value / math.sqrt((high * high - low) / (2.0 * math.log(high)))


def linear_ramp(count):
    return (1.0 + 2.0 * jnp.arange(count, dtype=jnp.float32) / count) / math.sqrt(13.0 / 3.0)


def draw_patches(key, part):
    key = jax.random.fold_in(key, 11)
    key_values, key_common, key_tokens, key_features = jax.random.split(key, 4)
    own = jnp.clip(jax.random.normal(key_values, (IMAGES, SEQ, D), jnp.float32), -4.0, 4.0)
    common = jnp.clip(jax.random.normal(key_common, (IMAGES, 1, D), jnp.float32), -4.0, 4.0)
    tokens = log_scales(key_tokens, (IMAGES, SEQ, 1), 1.0, 10.0)
    features = log_scales(key_features, (D,), 1.0, 10.0)
    values = 0.6 * common + 0.8 * own
    result = values * tokens * features * linear_ramp(D)
    return jnp.clip(result, -30.0, 30.0).astype(jnp.bfloat16)


def draw_out_grads(key, part):
    key = jax.random.fold_in(key, 23)
    key_values = jax.random.fold_in(key, 0)
    key_tokens = jax.random.fold_in(key, 2)
    key_columns = jax.random.fold_in(key, 3)
    key_images = jax.random.fold_in(key, 4)
    key_common = jax.random.fold_in(key, 5)
    offsets = jax.random.uniform(key_images, (IMAGES,), jnp.float32)
    images = jnp.exp(math.log(16.0) * (jnp.arange(IMAGES, dtype=jnp.float32) + offsets) / IMAGES)
    own = jnp.clip(jax.random.normal(key_values, (IMAGES, SEQ, HID), jnp.float32), -4.0, 4.0)
    common = jnp.clip(jax.random.normal(key_common, (IMAGES, 1, HID), jnp.float32), -4.0, 4.0)
    values = 0.6 * common + 0.8 * own
    tokens = log_scales(key_tokens, (IMAGES, SEQ, 1), 1.0, 10.0)
    columns = log_scales(key_columns, (HID,), 1.0, 10.0)
    result = values * tokens * columns * linear_ramp(HID) * images[:, None, None] / SEQ
    return jnp.clip(result, -8.0, 8.0).astype(jnp.bfloat16)


def setup_inputs(seed: int = 0) -> dict:
    arg_keys = jax.random.split(jax.random.key(seed), 3)
    return {
        "patches": draw_patches(jax.random.fold_in(arg_keys[2], 71), 0),
        "out_grads": draw_out_grads(jax.random.fold_in(arg_keys[2], 71), 0),
    }


def reference(patches, out_grads):
    x_float = patches.astype(jnp.float32)
    g_float = out_grads.astype(jnp.float32)
    gram_in = jnp.einsum('bsd,btd->bst', x_float, x_float, precision=lax.Precision.HIGHEST)
    gram_out = jnp.einsum('bsh,bth->bst', g_float, g_float, precision=lax.Precision.HIGHEST)
    squares = lax.optimization_barrier(jnp.sum(gram_in * gram_out, axis=(1, 2)))
    norms = jnp.sqrt(squares) / math.sqrt(D * HID)
    scale = 1.0 / jnp.maximum(norms, 1.0)
    flat_x = x_float.reshape(-1, D)
    flat_g = (g_float * scale[:, None, None]).reshape(-1, HID)
    clipped = jnp.dot(flat_x.T, flat_g, precision=lax.Precision.HIGHEST)
    return (clipped, norms)
```

```python
import functools
import math

import jax
import jax.numpy as jnp
from jax import lax
from jax.experimental import pallas as pl
from jax.experimental.pallas import tpu as pltpu
from jax.sharding import PartitionSpec as P

D = 6144
HID = 24576
IMAGES = 16
SEQ = 256
CHUNKS = 8
ROWS = 16
WIDTH = 192
COLS = 3072
HALF = COLS // 2
QUARTER = HALF // 2
TILE = 256
BATCHES = ((0, 1, 2), (3, 4), (5, 6), (7,))
F32 = jnp.float32


def kernel(
    x_ref, g_ref, out_ref, norms_ref,
    gbuf, own, sib, xbuf, xt, tiles, scale, sum_z, sum_y, sum_x,
    local_sem, swap_send, swap_recv, x_send, x_recv,
    ici_send, ici_recv, sib_send, sib_recv,
    z_send, z_recv, y_send, y_recv, w_send, w_recv,
):
    row, z = lax.axis_index("row"), lax.axis_index("col")
    core, y, x = lax.rem(row, 2), lax.rem(row // 2, 4), row // 8

    def at(px, py, pc):
        return {"row": (px * 4 + py) * 2 + pc}

    def up(v, d, n=4):
        return lax.rem(v + d + n, n)

    sibling = at(x, y, 1 - core)
    along_z = [{"col": up(z, d, 8)} for d in range(1, 8)]
    along_yc = [
        (up(y, dy), lax.rem(core + dc, 2))
        for dy in range(4) for dc in range(2) if dy or dc
    ]
    along_x = [up(x, d) for d in range(1, 4)]
    ahead = [at(up(x, 1), y, core), at(up(x, -1), y, core), at(x, up(y, 1), core), at(x, up(y, -1), core)]

    load_g = pltpu.make_async_copy(g_ref, own, local_sem.at[0])
    load_x = pltpu.make_async_copy(x_ref, xbuf.at[z], local_sem.at[1])
    load_g.start()
    load_x.start()

    barrier = pltpu.get_barrier_semaphore()
    peers = along_z + [at(x, py, pc) for py, pc in along_yc] + [at(px, y, core) for px in along_x]
    for peer in peers:
        pl.semaphore_signal(barrier, inc=1, device_id=peer)
    pl.semaphore_wait(barrier, len(peers))

    sends = []

    def send(src, dst, s, r, to, keep=True):
        copy = pltpu.make_async_remote_copy(src, dst, s, r, device_id=to)
        copy.start()
        if keep:
            sends.append(copy)

    def arrived(block, s, r, to):
        pltpu.make_async_remote_copy(block, block, s, r, device_id=to).wait_recv()

    parts = (pl.ds(0, ROWS), pl.ds(ROWS, (CHUNKS - 1) * ROWS))
    for i, rows in enumerate(parts):
        send(g_ref.at[rows], sib.at[rows], swap_send.at[i], swap_recv.at[i], sibling)

    def x_step(s):
        for way, last in ((0, 4), (1, 3)):
            sign = 1 if way == 0 else -1
            if 0 < s <= last:
                block = xbuf.at[up(z, -sign * s, 8)]
                arrived(block, x_send.at[way, s - 1], x_recv.at[way, s - 1], {"col": up(z, sign, 8)})
            if s < last:
                here = up(z, -sign * s, 8)
                src = x_ref if s == 0 else xbuf.at[here]
                send(src, xbuf.at[here], x_send.at[way, s], x_recv.at[way, s], {"col": up(z, sign, 8)})

    def merge(j):
        rows = pl.ds(j * ROWS, ROWS)
        for c in range(0, COLS, 768):
            cols = pl.ds(c, 768)
            a = own[rows, cols].astype(F32)
            b = sib[rows, cols].astype(F32)
            first = jnp.where(core == 0, a[:8], b[8:])
            second = jnp.where(core == 0, b[:8], a[8:])
            both = jnp.concatenate([first, second], axis=0).astype(jnp.bfloat16)
            gbuf[2 * j + core, x, y, :, cols] = both

    def part(b, half, px, py, piece=None):
        start, size = half * HALF, HALF
        if piece is not None:
            start, size = start + piece * QUARTER, QUARTER
        return gbuf.at[b, px, py, :, pl.ds(start, size)]

    everything = slice(None)

    def block(j, half, stage, way, behind):
        b = 2 * j + core
        sign = 1 if way % 2 == 0 else -1
        piece = None if stage % 2 == 0 else way % 2
        if way < 2:
            px, py = up(x, -sign * behind), y
        else:
            px, py = x, up(y, -sign * behind)
        if stage >= 2:
            if half == 0:
                px = everything
            else:
                py = everything
        return part(b, half, px, py, piece)

    def routes(stage):
        for half in range(2):
            along = half if stage < 2 else 1 - half
            for way in (2 * along, 2 * along + 1):
                yield half, way

    def put(j, stage):
        for half, way in routes(stage):
            src = block(j, half, stage, way, stage % 2)
            slot = stage * 4 + way
            send(src, src, ici_send.at[j, slot], ici_recv.at[j, slot], ahead[way])

    def take(j, stage):
        for half, way in routes(stage):
            slot = stage * 4 + way
            arrived(block(j, half, stage, way, 1 + stage % 2), ici_send.at[j, slot], ici_recv.at[j, slot], ahead[way])

    def strip(b, half, d):
        if half == 0:
            return part(b, 0, everything, up(y, d))
        return part(b, 1, up(x, d), everything)

    def share(j, ds):
        for half in range(2):
            for d in ds:
                slot = half * 4 + d
                src = strip(2 * j + core, half, d)
                send(src, src, sib_send.at[j, slot], sib_recv.at[j, slot], sibling)

    def shared(j):
        for half in range(2):
            for d in range(4):
                slot = half * 4 + d
                arrived(strip(2 * j + 1 - core, half, d), sib_send.at[j, slot], sib_recv.at[j, slot], sibling)

    def s0(j):
        put(j, 0)

    def s1(j):
        take(j, 0)
        put(j, 1)

    def s2(j):
        take(j, 1)
        put(j, 2)
        share(j, (0,))

    def s3(j):
        take(j, 2)
        put(j, 3)
        share(j, (1, 3))

    def s4(j):
        take(j, 3)
        share(j, (2,))

    def turn(b, carry):
        xt[b] = xbuf[:, b].reshape(SEQ, WIDTH).astype(F32).T.astype(jnp.bfloat16)
        return carry

    def product(b, cols):
        g = gbuf[b, :, :, :, cols].reshape(SEQ, TILE)
        return jnp.dot(xt[b], g, preferred_element_type=F32)

    def squares(b, slot):
        def body(n, acc):
            cols = pl.ds(pl.multiple_of(n * TILE, TILE), TILE)
            t = product(b, cols)
            if slot is not None:
                tiles[slot, :, cols] = t
            s = (t * t).reshape(WIDTH // 8, 8, TILE).sum(axis=0)
            return acc + s[:, :128] + s[:, 128:]

        acc = lax.fori_loop(0, COLS // TILE, body, jnp.zeros((8, 128), F32))
        return jnp.sum(acc, axis=0, keepdims=True)

    def images(k):
        return [b for j in BATCHES[k] for b in (2 * j, 2 * j + 1)]

    def compute(j):
        k = [i for i, batch in enumerate(BATCHES) if j in batch][0]
        for b in (2 * j, 2 * j + 1):
            slot = b - 14 if k == len(BATCHES) - 1 else None
            n = images(k).index(b)
            sum_z[k, z, n : n + 1, :] = squares(b, slot)
        if j == BATCHES[k][0] and len(images(k)) < 8:
            sum_z[k, z, len(images(k)) :, :] = jnp.zeros((8 - len(images(k)), 128), F32)

    def reduce_z(k):
        mine = sum_z.at[k, z]
        for i, peer in enumerate(along_z):
            send(mine, mine, z_send.at[k, i], z_recv.at[k, z], peer)

    def reduce_y(k):
        for i, peer in enumerate(along_z):
            arrived(sum_z.at[k, peer["col"]], z_send.at[k, i], z_recv.at[k, peer["col"]], peer)
        me = y * 2 + core
        sum_y[k, me] = jnp.sum(sum_z[k], axis=0)
        mine = sum_y.at[k, me]
        for i, (py, pc) in enumerate(along_yc):
            send(mine, mine, y_send.at[k, i], y_recv.at[k, me], at(x, py, pc))

    def reduce_x(k):
        for i, (py, pc) in enumerate(along_yc):
            it = py * 2 + pc
            arrived(sum_y.at[k, it], y_send.at[k, i], y_recv.at[k, it], at(x, py, pc))
        sum_x[k, x] = jnp.sum(sum_y[k], axis=0)
        mine = sum_x.at[k, x]
        for i, px in enumerate(along_x):
            send(mine, mine, w_send.at[k, i], w_recv.at[k, x], at(px, y, core))

    def reduced(k):
        for i, px in enumerate(along_x):
            arrived(sum_x.at[k, px], w_send.at[k, i], w_recv.at[k, px], at(px, y, core))
        total = jnp.sum(jnp.sum(sum_x[k], axis=0), axis=1, keepdims=True)
        norm = jnp.sqrt(total) / math.sqrt(D * HID)
        norm = jnp.broadcast_to(norm, (8, TILE))
        first, count = images(k)[0], len(images(k))
        norms_ref[first : first + count, :] = norm[:count, :128]
        scale[first : first + count, :] = (1.0 / jnp.maximum(norm, 1.0))[:count]

    def accumulate(bs):
        def body(n, carry):
            cols = pl.ds(pl.multiple_of(n * TILE, TILE), TILE)
            acc = out_ref[:, cols] if bs[0] else jnp.zeros((WIDTH, TILE), F32)
            for b in bs:
                acc = acc + scale[b : b + 1, :] * product(b, cols)
            out_ref[:, cols] = acc
            return carry

        lax.fori_loop(0, COLS // TILE, body, 0)

    def finish():
        def body(n, carry):
            cols = pl.ds(pl.multiple_of(n * TILE, TILE), TILE)
            acc = out_ref[:, cols]
            for b in (14, 15):
                acc = acc + scale[b : b + 1, :] * tiles[b - 14, :, cols]
            out_ref[:, cols] = acc
            return carry

        lax.fori_loop(0, COLS // TILE, body, 0)

    x_step(0)
    load_g.wait()
    load_x.wait()
    arrived(sib.at[parts[0]], swap_send.at[0], swap_recv.at[0], sibling)
    merge(0)
    s0(0)
    arrived(sib.at[parts[1]], swap_send.at[1], swap_recv.at[1], sibling)
    merge(1)
    s0(1)
    for j in range(2, CHUNKS):
        merge(j)
    s1(0)
    s2(0)
    s1(1)
    x_step(1)

    for i in range(CHUNKS):
        if i + 2 < CHUNKS:
            s0(i + 2)
        if i + 1 < CHUNKS:
            s2(i + 1)
        if i == 1:
            x_step(3)
        if i == 2:
            x_step(4)
            lax.fori_loop(0, IMAGES, turn, 0)
            shared(0)
            compute(0)
        s3(i)
        if i == 0:
            x_step(2)
        if i + 2 < CHUNKS:
            s1(i + 2)
        if i == 4:
            reduce_y(0)
        if i == 6:
            reduce_y(1)
        s4(i)
        if i >= 2:
            shared(i - 1)
            compute(i - 1)
        if i == 3:
            reduce_z(0)
        if i == 4:
            reduce_x(0)
        if i == 5:
            reduce_z(1)
            reduced(0)
            accumulate((0, 1, 2, 3, 4, 5))
        if i == 6:
            reduce_x(1)
    reduce_z(2)
    reduced(1)
    reduce_y(2)
    accumulate((6, 7, 8, 9))
    reduce_x(2)
    shared(7)
    compute(7)
    reduce_z(3)
    reduced(2)
    accumulate((10, 11, 12, 13))
    reduce_y(3)
    reduce_x(3)
    for copy in sends:
        copy.wait_send()
    reduced(3)
    finish()


def shards(patches, out_grads):
    g = out_grads.reshape(CHUNKS * ROWS, COLS)
    bf16 = jnp.bfloat16
    dma = pltpu.SemaphoreType.DMA
    nb = len(BATCHES)
    clipped, norms = pl.pallas_call(
        kernel,
        out_shape=(
            jax.ShapeDtypeStruct((WIDTH, COLS), F32),
            jax.ShapeDtypeStruct((IMAGES, 128), F32),
        ),
        in_specs=[pl.BlockSpec(memory_space=pl.ANY)] * 2,
        out_specs=(pl.BlockSpec(memory_space=pltpu.VMEM), pl.BlockSpec(memory_space=pltpu.VMEM)),
        scratch_shapes=[
            pltpu.VMEM((IMAGES, 4, 4, ROWS, COLS), bf16),
            pltpu.VMEM((CHUNKS * ROWS, COLS), bf16),
            pltpu.VMEM((CHUNKS * ROWS, COLS), bf16),
            pltpu.VMEM((8, IMAGES, 32, WIDTH), bf16),
            pltpu.VMEM((IMAGES, WIDTH, SEQ), bf16),
            pltpu.VMEM((2, WIDTH, COLS), F32),
            pltpu.VMEM((IMAGES, TILE), F32),
            pltpu.VMEM((nb, 8, 8, 128), F32),
            pltpu.VMEM((nb, 8, 8, 128), F32),
            pltpu.VMEM((nb, 4, 8, 128), F32),
            dma((2,)),
            dma((2,)), dma((2,)),
            dma((2, 4)), dma((2, 4)),
            dma((CHUNKS, 16)), dma((CHUNKS, 16)),
            dma((CHUNKS, 8)), dma((CHUNKS, 8)),
            dma((nb, 7)), dma((nb, 8)),
            dma((nb, 7)), dma((nb, 8)),
            dma((nb, 3)), dma((nb, 4)),
        ],
        compiler_params=pltpu.CompilerParams(
            collective_id=0, has_side_effects=True, vmem_limit_bytes=56 * 1024 * 1024
        ),
    )(patches, g)
    return (clipped, norms[:, 0])


def solution(mesh):
    in_specs = (P(None, "col", "row"), P(None, "row", "col"))
    out_specs = (P("row", "col"), P())
    return jax.shard_map(shards, mesh=mesh, in_specs=in_specs, out_specs=out_specs, check_vma=False)
```

```python
import itertools
import math

import jax
import jax.numpy as jnp
from jax import lax
from jax.experimental import pallas as pl
from jax.experimental.pallas import tpu as pltpu
from jax.sharding import PartitionSpec as P

D = 6144
HID = 24576
IMAGES = 16
SEQ = 256
CHUNKS = 8
ROWS = 16
WIDTH = 192
COLS = 3072
HALF = COLS // 2
QUARTER = HALF // 2
TILE = 256
BATCHES = ((0, 1, 2, 3), (4, 5), (6, 7))
F32 = jnp.float32


def kernel(
    x_ref, g_ref, out_ref, norms_ref,
    gbuf, own, sib, xbuf, xt, xt_first, tiles, scale, sum_zc, sum_xy,
    local_sem, swap_send, swap_recv, x_send, x_recv,
    ici_send, ici_recv, sib_send, sib_recv,
    zc_send, zc_recv, xy_send, xy_recv,
):
    row, z = lax.axis_index("row"), lax.axis_index("col")
    core, y, x = lax.rem(row, 2), lax.rem(row // 2, 4), row // 8

    def at(px, py, pc):
        return {"row": (px * 4 + py) * 2 + pc}

    def up(v, d, n=4):
        return lax.rem(v + d + n, n)

    sibling = at(x, y, 1 - core)
    along_zc = [
        (up(z, dz, 8), lax.rem(core + dc, 2))
        for dz, dc in sorted(itertools.product(range(8), range(2)), key=lambda d: -min(d[0], 8 - d[0]) - d[1])
        if dz or dc
    ]
    along_xy = [
        (up(x, dx), up(y, dy))
        for dx, dy in sorted(itertools.product(range(4), range(4)), key=lambda d: -min(d[0], 4 - d[0]) - min(d[1], 4 - d[1]))
        if dx or dy
    ]
    ahead = [at(up(x, 1), y, core), at(up(x, -1), y, core), at(x, up(y, 1), core), at(x, up(y, -1), core)]

    load_g = pltpu.make_async_copy(g_ref, own, local_sem.at[0])
    load_x = pltpu.make_async_copy(x_ref, xbuf.at[z], local_sem.at[1])
    load_first = pltpu.make_async_copy(g_ref.at[pl.ds(0, ROWS)], gbuf.at[core, x, y], local_sem.at[2])
    load_g.start()
    load_x.start()
    load_first.start()

    barrier = pltpu.get_barrier_semaphore()
    peers = ahead + [{"col": up(z, 1, 8)}, {"col": up(z, -1, 8)}, sibling]
    for peer in peers:
        pl.semaphore_signal(barrier, inc=1, device_id=peer)
    pl.semaphore_wait(barrier, len(peers))

    sends = []

    def send(src, dst, s, r, to, keep=True):
        copy = pltpu.make_async_remote_copy(src, dst, s, r, device_id=to)
        copy.start()
        if keep:
            sends.append(copy)

    def arrived(block, s, r, to):
        pltpu.make_async_remote_copy(block, block, s, r, device_id=to).wait_recv()

    def swap():
        rows = pl.ds(ROWS, (CHUNKS - 1) * ROWS)
        send(g_ref.at[rows], sib.at[rows], swap_send.at[0], swap_recv.at[0], sibling)

    def x_step(s):
        for way, last in ((0, 4), (1, 3)):
            sign = 1 if way == 0 else -1
            if 0 < s <= last:
                block = xbuf.at[up(z, -sign * s, 8)]
                arrived(block, x_send.at[way, s - 1], x_recv.at[way, s - 1], {"col": up(z, sign, 8)})
            if s < last:
                here = up(z, -sign * s, 8)
                src = x_ref if s == 0 else xbuf.at[here]
                send(src, xbuf.at[here], x_send.at[way, s], x_recv.at[way, s], {"col": up(z, sign, 8)})

    def merge(j):
        rows = pl.ds(j * ROWS, ROWS)
        for c in range(0, COLS, 768):
            cols = pl.ds(c, 768)
            a = own[rows, cols].astype(F32)
            b = sib[rows, cols].astype(F32)
            first = jnp.where(core == 0, a[:8], b[8:])
            second = jnp.where(core == 0, b[:8], a[8:])
            both = jnp.concatenate([first, second], axis=0).astype(jnp.bfloat16)
            gbuf[2 * j + core, x, y, :, cols] = both

    def part(b, half, px, py, piece=None):
        start, size = half * HALF, HALF
        if piece is not None:
            start, size = start + piece * QUARTER, QUARTER
        return gbuf.at[b, px, py, :, pl.ds(start, size)]

    everything = slice(None)

    def block(j, half, stage, way, behind):
        b = 2 * j + core
        sign = 1 if way % 2 == 0 else -1
        piece = None if stage % 2 == 0 else way % 2
        if way < 2:
            px, py = up(x, -sign * behind), y
        else:
            px, py = x, up(y, -sign * behind)
        if stage >= 2:
            if half == 0:
                px = everything
            else:
                py = everything
        return part(b, half, px, py, piece)

    def routes(stage):
        for half in range(2):
            along = half if stage < 2 else 1 - half
            for way in (2 * along, 2 * along + 1):
                yield half, way

    def put(j, stage):
        for half, way in routes(stage):
            src = dst = block(j, half, stage, way, stage % 2)
            if j == 0 and stage == 0:
                src = g_ref.at[pl.ds(0, ROWS), pl.ds(half * HALF, HALF)]
            slot = stage * 4 + way
            send(src, dst, ici_send.at[j, slot], ici_recv.at[j, slot], ahead[way])

    def take(j, stage):
        for half, way in routes(stage):
            slot = stage * 4 + way
            arrived(block(j, half, stage, way, 1 + stage % 2), ici_send.at[j, slot], ici_recv.at[j, slot], ahead[way])

    def strip(b, half, d):
        if half == 0:
            return part(b, 0, everything, up(y, d))
        return part(b, 1, up(x, d), everything)

    def share(j, ds):
        for half in range(2):
            for d in ds:
                slot = half * 4 + d
                src = strip(2 * j + core, half, d)
                send(src, src, sib_send.at[j, slot], sib_recv.at[j, slot], sibling)

    def shared(j):
        for half in range(2):
            for d in range(4):
                slot = half * 4 + d
                arrived(strip(2 * j + 1 - core, half, d), sib_send.at[j, slot], sib_recv.at[j, slot], sibling)

    def s0(j):
        put(j, 0)

    def s1(j):
        take(j, 0)
        put(j, 1)

    def s2(j):
        take(j, 1)
        put(j, 2)
        share(j, (0,))

    def s3(j):
        take(j, 2)
        put(j, 3)
        share(j, (1, 3))

    def s4(j):
        take(j, 3)
        share(j, (2,))

    def turn(b, carry):
        xt[b] = xbuf[:, b].reshape(SEQ, WIDTH).astype(F32).T.astype(jnp.bfloat16)
        return carry

    def turn_first():
        for b in range(2):
            halves = xbuf[:, b].reshape(ROWS, 2, 8, WIDTH).astype(F32)
            nothing = jnp.zeros((ROWS, 8, WIDTH), F32)
            for h in range(2):
                pair = [halves[:, h], nothing] if b == 0 else [nothing, halves[:, h]]
                rows = jnp.stack(pair, axis=1).reshape(SEQ, WIDTH)
                xt_first[b, :, h * SEQ : (h + 1) * SEQ] = rows.T.astype(jnp.bfloat16)

    def product(b, cols):
        if isinstance(b, int) and b < 2:
            g = gbuf[0:2, :, :, :, cols].reshape(2 * SEQ, TILE)
            return jnp.dot(xt_first[b], g, preferred_element_type=F32)
        g = gbuf[b, :, :, :, cols].reshape(SEQ, TILE)
        return jnp.dot(xt[b], g, preferred_element_type=F32)

    def squares(b, slot):
        acc = jnp.zeros((8, 128), F32)
        for n in range(0, COLS, TILE):
            cols = pl.ds(n, TILE)
            t = product(b, cols)
            if slot is not None:
                tiles[slot, :, cols] = t
            s = (t * t).reshape(WIDTH // 8, 8, TILE).sum(axis=0)
            acc = acc + s[:, :128] + s[:, 128:]
        return jnp.sum(acc, axis=0, keepdims=True)

    def images(k):
        return [b for j in BATCHES[k] for b in (2 * j, 2 * j + 1)]

    def compute(j):
        k = [i for i, batch in enumerate(BATCHES) if j in batch][0]
        first, last = images(k)[0], k == len(BATCHES) - 1
        me = z * 2 + core
        if 2 * j == first and len(images(k)) < 8:
            sum_zc[k, me] = jnp.zeros((8, 128), F32)

        def one(b, carry):
            sum_zc[k, me, pl.ds(b - first, 1), :] = squares(b, b - first if last else None)
            return carry

        if j == 0:
            one(0, 0)
            one(1, 0)
        else:
            lax.fori_loop(2 * j, 2 * j + 2, one, 0)

    def reduce_zc(k):
        me = z * 2 + core
        mine = sum_zc.at[k, me]
        for i, (pz, pc) in enumerate(along_zc):
            send(mine, mine, zc_send.at[k, i], zc_recv.at[k, me], dict(at(x, y, pc), col=pz))

    def reduce_xy(k):
        for i, (pz, pc) in enumerate(along_zc):
            it = pz * 2 + pc
            arrived(sum_zc.at[k, it], zc_send.at[k, i], zc_recv.at[k, it], dict(at(x, y, pc), col=pz))
        me = x * 4 + y
        sum_xy[k, me] = jnp.sum(sum_zc[k], axis=0)
        mine = sum_xy.at[k, me]
        for i, (px, py) in enumerate(along_xy):
            send(mine, mine, xy_send.at[k, i], xy_recv.at[k, me], at(px, py, core))

    def reduced(k):
        for i, (px, py) in enumerate(along_xy):
            it = px * 4 + py
            arrived(sum_xy.at[k, it], xy_send.at[k, i], xy_recv.at[k, it], at(px, py, core))
        total = jnp.sum(jnp.sum(sum_xy[k], axis=0), axis=1, keepdims=True)
        norm = jnp.sqrt(total) / math.sqrt(D * HID)
        norm = jnp.broadcast_to(norm, (8, TILE))
        first, count = images(k)[0], len(images(k))
        norms_ref[first : first + count, :] = norm[:count, :128]
        scale[first : first + count, :] = (1.0 / jnp.maximum(norm, 1.0))[:count]

    def accumulate(first, count):
        def add(b):
            for n in range(0, COLS, TILE):
                cols = pl.ds(n, TILE)
                acc = scale[pl.ds(b, 1), :] * product(b, cols) + scale[pl.ds(b + 1, 1), :] * product(b + 1, cols)
                out_ref[:, cols] = acc if isinstance(b, int) and b == 0 else out_ref[:, cols] + acc

        def pair(i, carry):
            add(first + 2 * i)
            return carry

        if first == 0:
            add(0)
        lax.fori_loop(1 if first == 0 else 0, count // 2, pair, 0)

    def finish(first, count):
        for n in range(0, COLS, TILE):
            cols = pl.ds(n, TILE)
            acc = out_ref[:, cols]
            for i in range(count):
                acc = acc + scale[first + i : first + i + 1, :] * tiles[i, :, cols]
            out_ref[:, cols] = acc

    marks = [0]

    def flush():
        for copy in sends[: marks[-2] if len(marks) > 1 else 0]:
            if copy is not None:
                copy.wait_send()
        for i in range(marks[-2] if len(marks) > 1 else 0):
            sends[i] = None
        marks.append(len(sends))

    s0(0)
    swap()
    x_step(0)
    load_g.wait()
    load_x.wait()
    load_first.wait()
    rest = pl.ds(ROWS, (CHUNKS - 1) * ROWS)
    arrived(sib.at[rest], swap_send.at[0], swap_recv.at[0], sibling)
    for j in range(1, CHUNKS):
        merge(j)
        s0(j)
    for j in range(CHUNKS):
        s1(j)
        if j == 4:
            x_step(1)
    s2(0)
    s2(1)
    x_step(2)

    for i in range(CHUNKS):
        s3(i)
        if i + 2 < CHUNKS:
            s2(i + 2)
        if i == 0:
            x_step(3)
        if i == 5:
            reduce_xy(0)
        if i == 6:
            reduced(0)
            accumulate(0, 8)
        if i >= 1:
            s4(i - 1)
            if i == 1:
                x_step(4)
                turn_first()
                lax.fori_loop(2, IMAGES, turn, 0)
            shared(i - 1)
            compute(i - 1)
        if i == 4:
            reduce_zc(0)
        if i == 6:
            reduce_zc(1)
        if i == 7:
            reduce_xy(1)
        flush()
    s4(7)
    shared(7)
    compute(7)
    reduce_zc(2)
    reduced(1)
    accumulate(8, 4)
    reduce_xy(2)
    for copy in sends:
        if copy is not None:
            copy.wait_send()
    reduced(2)
    finish(12, 4)


def shards(patches, out_grads):
    g = out_grads.reshape(CHUNKS * ROWS, COLS)
    bf16 = jnp.bfloat16
    dma = pltpu.SemaphoreType.DMA
    nb = len(BATCHES)
    clipped, norms = pl.pallas_call(
        kernel,
        out_shape=(
            jax.ShapeDtypeStruct((WIDTH, COLS), F32),
            jax.ShapeDtypeStruct((IMAGES, 128), F32),
        ),
        in_specs=[pl.BlockSpec(memory_space=pltpu.HBM)] * 2,
        out_specs=(pl.BlockSpec(memory_space=pltpu.VMEM), pl.BlockSpec(memory_space=pltpu.VMEM)),
        scratch_shapes=[
            pltpu.VMEM((IMAGES, 4, 4, ROWS, COLS), bf16),
            pltpu.VMEM((CHUNKS * ROWS, COLS), bf16),
            pltpu.VMEM((CHUNKS * ROWS, COLS), bf16),
            pltpu.VMEM((8, IMAGES, 32, WIDTH), bf16),
            pltpu.VMEM((IMAGES, WIDTH, SEQ), bf16),
            pltpu.VMEM((2, WIDTH, 2 * SEQ), bf16),
            pltpu.VMEM((2 * len(BATCHES[-1]), WIDTH, COLS), F32),
            pltpu.VMEM((IMAGES, TILE), F32),
            pltpu.VMEM((nb, 16, 8, 128), F32),
            pltpu.VMEM((nb, 16, 8, 128), F32),
            dma((3,)),
            dma((1,)), dma((1,)),
            dma((2, 4)), dma((2, 4)),
            dma((CHUNKS, 16)), dma((CHUNKS, 16)),
            dma((CHUNKS, 8)), dma((CHUNKS, 8)),
            dma((nb, 15)), dma((nb, 16)),
            dma((nb, 15)), dma((nb, 16)),
        ],
        compiler_params=pltpu.CompilerParams(
            collective_id=0, has_side_effects=True, vmem_limit_bytes=46 * 1024 * 1024
        ),
    )(patches, g)
    return (clipped, norms[:, 0])


def solution(mesh):
    in_specs = (P(None, "col", "row"), P(None, "row", "col"))
    out_specs = (P("row", "col"), P())
    return jax.shard_map(shards, mesh=mesh, in_specs=in_specs, out_specs=out_specs, check_vma=False)
```

```python
import itertools
import math

import jax
import jax.numpy as jnp
from jax import lax
from jax.experimental import pallas as pl
from jax.experimental.pallas import tpu as pltpu
from jax.sharding import PartitionSpec as P

D = 6144
HID = 24576
IMAGES = 16
SEQ = 256
CHUNKS = 8
ROWS = 16
WIDTH = 192
COLS = 3072
HALF = COLS // 2
QUARTER = HALF // 2
TILE = 256
BATCHES = ((0, 1, 2, 3, 4, 5), (6, 7))
F32 = jnp.float32


def kernel(
    x_ref, g_ref, out_ref, norms_ref,
    gbuf, own, sib, xbuf, xt, xt_first, tiles, scale, sum_zc, sum_xy,
    local_sem, swap_send, swap_recv, x_send, x_recv,
    ici_send, ici_recv, sib_send, sib_recv,
    zc_send, zc_recv, xy_send, xy_recv,
):
    row, z = lax.axis_index("row"), lax.axis_index("col")
    core, y, x = lax.rem(row, 2), lax.rem(row // 2, 4), row // 8

    def at(px, py, pc):
        return {"row": (px * 4 + py) * 2 + pc}

    def up(v, d, n=4):
        return lax.rem(v + d + n, n)

    sibling = at(x, y, 1 - core)
    along_zc = [
        (up(z, dz, 8), lax.rem(core + dc, 2))
        for dz, dc in sorted(itertools.product(range(8), range(2)), key=lambda d: -min(d[0], 8 - d[0]) - d[1])
        if dz or dc
    ]
    along_xy = [
        (up(x, dx), up(y, dy))
        for dx, dy in sorted(itertools.product(range(4), range(4)), key=lambda d: -min(d[0], 4 - d[0]) - min(d[1], 4 - d[1]))
        if dx or dy
    ]
    ahead = [at(up(x, 1), y, core), at(up(x, -1), y, core), at(x, up(y, 1), core), at(x, up(y, -1), core)]

    load_g = pltpu.make_async_copy(g_ref, own, local_sem.at[0])
    load_x = pltpu.make_async_copy(x_ref, xbuf.at[z], local_sem.at[1])
    load_first = pltpu.make_async_copy(g_ref.at[pl.ds(0, ROWS)], gbuf.at[core, x, y], local_sem.at[2])
    load_g.start()
    load_x.start()
    load_first.start()

    barrier = pltpu.get_barrier_semaphore()
    peers = ahead + [{"col": up(z, 1, 8)}, {"col": up(z, -1, 8)}, sibling]
    for peer in peers:
        pl.semaphore_signal(barrier, inc=1, device_id=peer)
    pl.semaphore_wait(barrier, len(peers))

    sends = []

    def send(src, dst, s, r, to, keep=True):
        copy = pltpu.make_async_remote_copy(src, dst, s, r, device_id=to)
        copy.start()
        if keep:
            sends.append(copy)

    def arrived(block, s, r, to):
        pltpu.make_async_remote_copy(block, block, s, r, device_id=to).wait_recv()

    def swap():
        rows = pl.ds(ROWS, (CHUNKS - 1) * ROWS)
        send(g_ref.at[rows], sib.at[rows], swap_send.at[0], swap_recv.at[0], sibling)

    def x_step(s):
        for way, last in ((0, 4), (1, 3)):
            sign = 1 if way == 0 else -1
            if 0 < s <= last:
                block = xbuf.at[up(z, -sign * s, 8)]
                arrived(block, x_send.at[way, s - 1], x_recv.at[way, s - 1], {"col": up(z, sign, 8)})
            if s < last:
                here = up(z, -sign * s, 8)
                src = x_ref if s == 0 else xbuf.at[here]
                send(src, xbuf.at[here], x_send.at[way, s], x_recv.at[way, s], {"col": up(z, sign, 8)})

    def merge(j):
        rows = pl.ds(j * ROWS, ROWS)
        for c in range(0, COLS, 768):
            cols = pl.ds(c, 768)
            a = own[rows, cols].astype(F32)
            b = sib[rows, cols].astype(F32)
            first = jnp.where(core == 0, a[:8], b[8:])
            second = jnp.where(core == 0, b[:8], a[8:])
            both = jnp.concatenate([first, second], axis=0).astype(jnp.bfloat16)
            gbuf[2 * j + core, x, y, :, cols] = both

    def part(b, half, px, py, piece=None):
        start, size = half * HALF, HALF
        if piece is not None:
            start, size = start + piece * QUARTER, QUARTER
        return gbuf.at[b, px, py, :, pl.ds(start, size)]

    everything = slice(None)

    def block(j, half, stage, way, behind):
        b = 2 * j + core
        sign = 1 if way % 2 == 0 else -1
        piece = None if stage % 2 == 0 else way % 2
        if way < 2:
            px, py = up(x, -sign * behind), y
        else:
            px, py = x, up(y, -sign * behind)
        if stage >= 2:
            if half == 0:
                px = everything
            else:
                py = everything
        return part(b, half, px, py, piece)

    def routes(stage):
        for half in range(2):
            along = half if stage < 2 else 1 - half
            for way in (2 * along, 2 * along + 1):
                yield half, way

    def put(j, stage):
        for half, way in routes(stage):
            src = dst = block(j, half, stage, way, stage % 2)
            if j == 0 and stage == 0:
                src = g_ref.at[pl.ds(0, ROWS), pl.ds(half * HALF, HALF)]
            slot = stage * 4 + way
            send(src, dst, ici_send.at[j, slot], ici_recv.at[j, slot], ahead[way])

    def take(j, stage):
        for half, way in routes(stage):
            slot = stage * 4 + way
            arrived(block(j, half, stage, way, 1 + stage % 2), ici_send.at[j, slot], ici_recv.at[j, slot], ahead[way])

    def strip(b, half, d):
        if half == 0:
            return part(b, 0, everything, up(y, d))
        return part(b, 1, up(x, d), everything)

    def share(j, ds):
        for half in range(2):
            for d in ds:
                slot = half * 4 + d
                src = strip(2 * j + core, half, d)
                send(src, src, sib_send.at[j, slot], sib_recv.at[j, slot], sibling)

    def shared(j):
        for half in range(2):
            for d in range(4):
                slot = half * 4 + d
                arrived(strip(2 * j + 1 - core, half, d), sib_send.at[j, slot], sib_recv.at[j, slot], sibling)

    def s0(j):
        put(j, 0)

    def s1(j):
        take(j, 0)
        put(j, 1)

    def s2(j):
        take(j, 1)
        put(j, 2)
        share(j, (0,))

    def s3(j):
        take(j, 2)
        put(j, 3)
        share(j, (1, 3))

    def s4(j):
        take(j, 3)
        share(j, (2,))

    def turn(b, carry):
        xt[b] = xbuf[:, b].reshape(SEQ, WIDTH).astype(F32).T.astype(jnp.bfloat16)
        return carry

    def turn_first():
        for b in range(2):
            halves = xbuf[:, b].reshape(ROWS, 2, 8, WIDTH).astype(F32)
            nothing = jnp.zeros((ROWS, 8, WIDTH), F32)
            for h in range(2):
                pair = [halves[:, h], nothing] if b == 0 else [nothing, halves[:, h]]
                rows = jnp.stack(pair, axis=1).reshape(SEQ, WIDTH)
                xt_first[b, :, h * SEQ : (h + 1) * SEQ] = rows.T.astype(jnp.bfloat16)

    def product(b, cols):
        if isinstance(b, int) and b < 2:
            g = gbuf[0:2, :, :, :, cols].reshape(2 * SEQ, TILE)
            return jnp.dot(xt_first[b], g, preferred_element_type=F32)
        g = gbuf[b, :, :, :, cols].reshape(SEQ, TILE)
        return jnp.dot(xt[b], g, preferred_element_type=F32)

    def squares(b, slot):
        acc = jnp.zeros((8, 128), F32)
        for n in range(0, COLS, TILE):
            cols = pl.ds(n, TILE)
            t = product(b, cols)
            if slot is not None:
                tiles[slot, :, cols] = t
            s = (t * t).reshape(WIDTH // 8, 8, TILE).sum(axis=0)
            acc = acc + s[:, :128] + s[:, 128:]
        return jnp.sum(acc, axis=0, keepdims=True)

    def images(k):
        return [b for j in BATCHES[k] for b in (2 * j, 2 * j + 1)]

    def compute(j, which=(0, 1)):
        k = [i for i, batch in enumerate(BATCHES) if j in batch][0]
        first, last = images(k)[0], k == len(BATCHES) - 1
        me = z * 2 + core

        def one(b, carry):
            sum_zc[k, me, pl.ds(b - first, 1), :] = squares(b, b - first if last else None)
            return carry

        if j == 0:
            one(0, 0)
            one(1, 0)
        elif len(which) == 2:
            lax.fori_loop(2 * j, 2 * j + 2, one, 0)
        else:
            one(2 * j + which[0], 0)

    def reduce_zc(k):
        me = z * 2 + core
        mine = sum_zc.at[k, me]
        for i, (pz, pc) in enumerate(along_zc):
            send(mine, mine, zc_send.at[k, i], zc_recv.at[k, me], dict(at(x, y, pc), col=pz))

    def reduce_xy(k):
        for i, (pz, pc) in enumerate(along_zc):
            it = pz * 2 + pc
            arrived(sum_zc.at[k, it], zc_send.at[k, i], zc_recv.at[k, it], dict(at(x, y, pc), col=pz))
        me = x * 4 + y
        sum_xy[k, me] = jnp.sum(sum_zc[k], axis=0)
        mine = sum_xy.at[k, me]
        for i, (px, py) in enumerate(along_xy):
            send(mine, mine, xy_send.at[k, i], xy_recv.at[k, me], at(px, py, core))

    def reduced(k):
        for i, (px, py) in enumerate(along_xy):
            it = px * 4 + py
            arrived(sum_xy.at[k, it], xy_send.at[k, i], xy_recv.at[k, it], at(px, py, core))
        total = jnp.sum(jnp.sum(sum_xy[k], axis=0), axis=1, keepdims=True)
        norm = jnp.sqrt(total) / math.sqrt(D * HID)
        norm = jnp.broadcast_to(norm, (16, TILE))
        first, count = images(k)[0], len(images(k))
        norms_ref[first : first + count, :] = norm[:count, :128]
        scale[first : first + count, :] = (1.0 / jnp.maximum(norm, 1.0))[:count]

    def accumulate(first, count):
        def add(b):
            for n in range(0, COLS, TILE):
                cols = pl.ds(n, TILE)
                acc = scale[pl.ds(b, 1), :] * product(b, cols) + scale[pl.ds(b + 1, 1), :] * product(b + 1, cols)
                out_ref[:, cols] = acc if isinstance(b, int) and b == 0 else out_ref[:, cols] + acc

        def pair(i, carry):
            add(first + 2 * i)
            return carry

        if first == 0:
            add(0)
        lax.fori_loop(1 if first == 0 else 0, count // 2, pair, 0)

    def finish(first, count):
        for n in range(0, COLS, TILE):
            cols = pl.ds(n, TILE)
            acc = out_ref[:, cols]
            for i in range(count):
                acc = acc + scale[first + i : first + i + 1, :] * tiles[i, :, cols]
            out_ref[:, cols] = acc

    marks = [0]

    def flush():
        for copy in sends[: marks[-2] if len(marks) > 1 else 0]:
            if copy is not None:
                copy.wait_send()
        for i in range(marks[-2] if len(marks) > 1 else 0):
            sends[i] = None
        marks.append(len(sends))

    s0(0)
    swap()
    x_step(0)
    for k in range(len(BATCHES)):
        sum_zc[k, z * 2 + core] = jnp.zeros((16, 128), F32)
    load_g.wait()
    load_x.wait()
    load_first.wait()
    rest = pl.ds(ROWS, (CHUNKS - 1) * ROWS)
    arrived(sib.at[rest], swap_send.at[0], swap_recv.at[0], sibling)
    for j in range(1, CHUNKS):
        merge(j)
        s0(j)
    for j in range(CHUNKS):
        s1(j)
        if j == 4:
            x_step(1)
    s2(0)
    s2(1)
    x_step(2)

    for i in range(CHUNKS):
        s3(i)
        if i + 2 < CHUNKS:
            s2(i + 2)
        if i == 0:
            x_step(3)
        if i >= 1:
            s4(i - 1)
            if i == 1:
                x_step(4)
                turn_first()
                lax.fori_loop(2, IMAGES, turn, 0)
            shared(i - 1)
            compute(i - 1)
        if i == 6:
            reduce_zc(0)
        flush()
    s4(7)
    reduce_xy(0)
    compute(7, (core,))
    shared(7)
    compute(7, (1 - core,))
    reduce_zc(1)
    reduced(0)
    accumulate(0, 12)
    reduce_xy(1)
    for copy in sends:
        if copy is not None:
            copy.wait_send()
    reduced(1)
    finish(12, 4)


def shards(patches, out_grads):
    g = out_grads.reshape(CHUNKS * ROWS, COLS)
    bf16 = jnp.bfloat16
    dma = pltpu.SemaphoreType.DMA
    nb = len(BATCHES)
    clipped, norms = pl.pallas_call(
        kernel,
        out_shape=(
            jax.ShapeDtypeStruct((WIDTH, COLS), F32),
            jax.ShapeDtypeStruct((IMAGES, 128), F32),
        ),
        in_specs=[pl.BlockSpec(memory_space=pltpu.HBM)] * 2,
        out_specs=(pl.BlockSpec(memory_space=pltpu.VMEM), pl.BlockSpec(memory_space=pltpu.VMEM)),
        scratch_shapes=[
            pltpu.VMEM((IMAGES, 4, 4, ROWS, COLS), bf16),
            pltpu.VMEM((CHUNKS * ROWS, COLS), bf16),
            pltpu.VMEM((CHUNKS * ROWS, COLS), bf16),
            pltpu.VMEM((8, IMAGES, 32, WIDTH), bf16),
            pltpu.VMEM((IMAGES, WIDTH, SEQ), bf16),
            pltpu.VMEM((2, WIDTH, 2 * SEQ), bf16),
            pltpu.VMEM((2 * len(BATCHES[-1]), WIDTH, COLS), F32),
            pltpu.VMEM((IMAGES, TILE), F32),
            pltpu.VMEM((nb, 16, 16, 128), F32),
            pltpu.VMEM((nb, 16, 16, 128), F32),
            dma((3,)),
            dma((1,)), dma((1,)),
            dma((2, 4)), dma((2, 4)),
            dma((CHUNKS, 16)), dma((CHUNKS, 16)),
            dma((CHUNKS, 8)), dma((CHUNKS, 8)),
            dma((nb, 15)), dma((nb, 16)),
            dma((nb, 15)), dma((nb, 16)),
        ],
        compiler_params=pltpu.CompilerParams(
            collective_id=0, has_side_effects=True, vmem_limit_bytes=46 * 1024 * 1024
        ),
    )(patches, g)
    return (clipped, norms[:, 0])


def solution(mesh):
    in_specs = (P(None, "col", "row"), P(None, "row", "col"))
    out_specs = (P("row", "col"), P())
    return jax.shard_map(shards, mesh=mesh, in_specs=in_specs, out_specs=out_specs, check_vma=False)
```

```python
import itertools
import math

import jax
import jax.numpy as jnp
from jax import lax
from jax.experimental import pallas as pl
from jax.experimental.pallas import tpu as pltpu
from jax.sharding import PartitionSpec as P

D = 6144
HID = 24576
IMAGES = 16
SEQ = 256
CHUNKS = 8
COARSE = 6
ROWS = 16
WIDTH = 192
COLS = 3072
HALF = COLS // 2
QUARTER = HALF // 2
TILE = 256
BATCHES = ((0, 1, 2, 3, 4), (5, 6, 7))
F32 = jnp.float32


def kernel(
    x_ref, g_ref, out_ref, norms_ref,
    gbuf, own, sib, xbuf, xt, xt_first, xt_twin, tiles, scale, sum_zc, sum_xy,
    local_sem, swap_send, swap_recv, x_send, x_recv,
    ici_send, ici_recv, sib_send, sib_recv,
    zc_send, zc_recv, xy_send, xy_recv, twin_send, twin_recv,
):
    row, z = lax.axis_index("row"), lax.axis_index("col")
    core, y, x = lax.rem(row, 2), lax.rem(row // 2, 4), row // 8

    def at(px, py, pc):
        return {"row": (px * 4 + py) * 2 + pc}

    def up(v, d, n=4):
        return lax.rem(v + d + n, n)

    sibling = at(x, y, 1 - core)
    along_zc = [
        (up(z, dz, 8), lax.rem(core + dc, 2))
        for dz, dc in sorted(itertools.product(range(8), range(2)), key=lambda d: -min(d[0], 8 - d[0]) - d[1])
        if dz or dc
    ]
    along_xy = [
        (up(x, dx), up(y, dy))
        for dx, dy in sorted(itertools.product(range(4), range(4)), key=lambda d: -min(d[0], 4 - d[0]) - min(d[1], 4 - d[1]))
        if dx or dy
    ]
    ahead = [at(up(x, 1), y, core), at(up(x, -1), y, core), at(x, up(y, 1), core), at(x, up(y, -1), core)]

    load_g = pltpu.make_async_copy(g_ref, own, local_sem.at[0])
    load_x = pltpu.make_async_copy(x_ref, xbuf.at[z], local_sem.at[1])
    load_first = pltpu.make_async_copy(g_ref.at[pl.ds(0, ROWS)], gbuf.at[core, x, y], local_sem.at[2])
    load_g.start()
    load_x.start()
    load_first.start()

    barrier = pltpu.get_barrier_semaphore()
    peers = ahead + [{"col": up(z, 1, 8)}, {"col": up(z, -1, 8)}, sibling]
    for peer in peers:
        pl.semaphore_signal(barrier, inc=1, device_id=peer)
    pl.semaphore_wait(barrier, len(peers))

    sends = []

    def send(src, dst, s, r, to, keep=True):
        copy = pltpu.make_async_remote_copy(src, dst, s, r, device_id=to)
        copy.start()
        if keep:
            sends.append(copy)

    def arrived(block, s, r, to):
        pltpu.make_async_remote_copy(block, block, s, r, device_id=to).wait_recv()

    def swap():
        rows = pl.ds(ROWS, (CHUNKS - 1) * ROWS)
        send(g_ref.at[rows], sib.at[rows], swap_send.at[0], swap_recv.at[0], sibling)

    def x_step(s):
        for way, last in ((0, 4), (1, 3)):
            sign = 1 if way == 0 else -1
            if 0 < s <= last:
                block = xbuf.at[up(z, -sign * s, 8)]
                arrived(block, x_send.at[way, s - 1], x_recv.at[way, s - 1], {"col": up(z, sign, 8)})
            if s < last:
                here = up(z, -sign * s, 8)
                src = x_ref if s == 0 else xbuf.at[here]
                send(src, xbuf.at[here], x_send.at[way, s], x_recv.at[way, s], {"col": up(z, sign, 8)})

    def merge(j):
        rows = pl.ds(j * ROWS, ROWS)
        for c in range(0, COLS, 768):
            cols = pl.ds(c, 768)
            a = own[rows, cols].astype(F32)
            b = sib[rows, cols].astype(F32)
            first = jnp.where(core == 0, a[:8], b[8:])
            second = jnp.where(core == 0, b[:8], a[8:])
            both = jnp.concatenate([first, second], axis=0).astype(jnp.bfloat16)
            gbuf[2 * j + core, x, y, :, cols] = both

    def part(b, half, px, py, piece=None):
        start, size = half * HALF, HALF
        if piece is not None:
            start, size = start + piece * QUARTER, QUARTER
        return gbuf.at[b, px, py, :, pl.ds(start, size)]

    everything = slice(None)

    def block(j, half, stage, way, behind):
        b = 2 * j + core
        sign = 1 if way % 2 == 0 else -1
        piece = None if stage % 2 == 0 else way % 2
        if way < 2:
            px, py = up(x, -sign * behind), y
        else:
            px, py = x, up(y, -sign * behind)
        if stage >= 2:
            if half == 0:
                px = everything
            else:
                py = everything
        return part(b, half, px, py, piece)

    def routes(stage):
        for half in range(2):
            along = half if stage < 2 else 1 - half
            for way in (2 * along, 2 * along + 1):
                yield half, way

    def put(j, stage):
        for half, way in routes(stage):
            src = dst = block(j, half, stage, way, stage % 2)
            if j == 0 and stage == 0:
                src = g_ref.at[pl.ds(0, ROWS), pl.ds(half * HALF, HALF)]
            slot = stage * 4 + way
            send(src, dst, ici_send.at[j, slot], ici_recv.at[j, slot], ahead[way])

    def take(j, stage):
        for half, way in routes(stage):
            slot = stage * 4 + way
            arrived(block(j, half, stage, way, 1 + stage % 2), ici_send.at[j, slot], ici_recv.at[j, slot], ahead[way])

    def strip(b, half, d):
        if half == 0:
            return part(b, 0, everything, up(y, d))
        return part(b, 1, up(x, d), everything)

    def share(j, ds):
        if j < COARSE:
            if 2 in ds:
                src = gbuf.at[2 * j + core]
                send(src, src, sib_send.at[j, 0], sib_recv.at[j, 0], sibling)
            return
        for half in range(2):
            for d in ds:
                slot = half * 4 + d
                src = strip(2 * j + core, half, d)
                send(src, src, sib_send.at[j, slot], sib_recv.at[j, slot], sibling)

    def shared(j):
        if j < COARSE:
            arrived(gbuf.at[2 * j + 1 - core], sib_send.at[j, 0], sib_recv.at[j, 0], sibling)
            return
        for half in range(2):
            for d in range(4):
                slot = half * 4 + d
                arrived(strip(2 * j + 1 - core, half, d), sib_send.at[j, slot], sib_recv.at[j, slot], sibling)

    def s0(j):
        put(j, 0)

    def s1(j):
        take(j, 0)
        put(j, 1)

    def s2(j):
        take(j, 1)
        put(j, 2)
        share(j, (0,))

    def s3(j):
        take(j, 2)
        put(j, 3)
        share(j, (1, 3))

    def s4(j):
        take(j, 3)
        share(j, (2,))

    def turn(b, carry):
        xt[b] = xbuf[:, b].reshape(SEQ, WIDTH).astype(F32).T.astype(jnp.bfloat16)
        return carry

    def turn_first():
        for b in range(2):
            halves = xbuf[:, b].reshape(ROWS, 2, 8, WIDTH).astype(F32)
            nothing = jnp.zeros((ROWS, 8, WIDTH), F32)
            for h in range(2):
                pair = [halves[:, h], nothing] if b == 0 else [nothing, halves[:, h]]
                rows = jnp.stack(pair, axis=1).reshape(SEQ, WIDTH)
                xt_first[b, :, h * SEQ : (h + 1) * SEQ] = rows.T.astype(jnp.bfloat16)

    def product(b, cols):
        if isinstance(b, int) and b < 2:
            g = gbuf[0:2, :, :, :, cols].reshape(2 * SEQ, TILE)
            return jnp.dot(xt_first[b], g, preferred_element_type=F32)
        g = gbuf[b, :, :, :, cols].reshape(SEQ, TILE)
        return jnp.dot(xt[b], g, preferred_element_type=F32)

    def squares(b, slot):
        acc = jnp.zeros((8, 128), F32)
        for n in range(0, COLS, TILE):
            cols = pl.ds(n, TILE)
            t = product(b, cols)
            if slot is not None:
                tiles[slot, :, cols] = t
            s = (t * t).reshape(WIDTH // 8, 8, TILE).sum(axis=0)
            acc = acc + s[:, :128] + s[:, 128:]
        return jnp.sum(acc, axis=0, keepdims=True)

    def images(k):
        return [b for j in BATCHES[k] for b in (2 * j, 2 * j + 1)]

    def compute(j):
        k = [i for i, batch in enumerate(BATCHES) if j in batch][0]
        first, last = images(k)[0], k == len(BATCHES) - 1
        me = z * 2 + core

        def one(b, carry):
            sum_zc[k, me, pl.ds(b - first, 1), :] = squares(b, b - first if last else None)
            return carry

        if j == 0:
            one(0, 0)
            one(1, 0)
        else:
            lax.fori_loop(2 * j, 2 * j + 2, one, 0)

    def compute_last():
        b = 2 * (CHUNKS - 1) + core
        arrived(xt_twin, twin_send.at[0], twin_recv.at[0], sibling)
        acc = jnp.zeros((8, 128), F32)
        for n in range(0, COLS, TILE):
            cols = pl.ds(n, TILE)
            g = gbuf[b, :, :, :, cols].reshape(SEQ, TILE)
            mine = jnp.dot(xt[b], g, preferred_element_type=F32)
            twin = jnp.dot(xt_twin[...], g, preferred_element_type=F32)
            tiles[4 + core, :, cols] = mine
            s = (mine * mine + twin * twin).reshape(WIDTH // 8, 8, TILE).sum(axis=0)
            acc = acc + s[:, :128] + s[:, 128:]
        sum_zc[1, z * 2 + core, pl.ds(4 + core, 1), :] = jnp.sum(acc, axis=0, keepdims=True)

    def tile_last():
        b = 2 * CHUNKS - 1 - core
        for n in range(0, COLS, TILE):
            cols = pl.ds(n, TILE)
            tiles[5 - core, :, cols] = product(b, cols)

    def reduce_zc(k):
        me = z * 2 + core
        mine = sum_zc.at[k, me]
        for i, (pz, pc) in enumerate(along_zc):
            send(mine, mine, zc_send.at[k, i], zc_recv.at[k, me], dict(at(x, y, pc), col=pz))

    def reduce_xy(k):
        for i, (pz, pc) in enumerate(along_zc):
            it = pz * 2 + pc
            arrived(sum_zc.at[k, it], zc_send.at[k, i], zc_recv.at[k, it], dict(at(x, y, pc), col=pz))
        me = x * 4 + y
        sum_xy[k, me] = jnp.sum(sum_zc[k], axis=0)
        mine = sum_xy.at[k, me]
        for i, (px, py) in enumerate(along_xy):
            send(mine, mine, xy_send.at[k, i], xy_recv.at[k, me], at(px, py, core))

    def reduced(k):
        for i, (px, py) in enumerate(along_xy):
            it = px * 4 + py
            arrived(sum_xy.at[k, it], xy_send.at[k, i], xy_recv.at[k, it], at(px, py, core))
        total = jnp.sum(jnp.sum(sum_xy[k], axis=0), axis=1, keepdims=True)
        norm = jnp.sqrt(total) / math.sqrt(D * HID)
        norm = jnp.broadcast_to(norm, (16, TILE))
        first, count = images(k)[0], len(images(k))
        norms_ref[first : first + count, :] = norm[:count, :128]
        scale[first : first + count, :] = (1.0 / jnp.maximum(norm, 1.0))[:count]

    def accumulate(first, count):
        def add(b):
            for n in range(0, COLS, TILE):
                cols = pl.ds(n, TILE)
                acc = scale[pl.ds(b, 1), :] * product(b, cols) + scale[pl.ds(b + 1, 1), :] * product(b + 1, cols)
                out_ref[:, cols] = acc if isinstance(b, int) and b == 0 else out_ref[:, cols] + acc

        def pair(i, carry):
            add(first + 2 * i)
            return carry

        if first == 0:
            add(0)
        lax.fori_loop(1 if first == 0 else 0, count // 2, pair, 0)

    def finish(first, count):
        for n in range(0, COLS, TILE):
            cols = pl.ds(n, TILE)
            acc = out_ref[:, cols]
            for i in range(count):
                acc = acc + scale[first + i : first + i + 1, :] * tiles[i, :, cols]
            out_ref[:, cols] = acc

    marks = [0]

    def flush():
        for copy in sends[: marks[-2] if len(marks) > 1 else 0]:
            if copy is not None:
                copy.wait_send()
        for i in range(marks[-2] if len(marks) > 1 else 0):
            sends[i] = None
        marks.append(len(sends))

    s0(0)
    swap()
    x_step(0)
    for k in range(len(BATCHES)):
        sum_zc[k, z * 2 + core] = jnp.zeros((16, 128), F32)
    load_g.wait()
    load_x.wait()
    load_first.wait()
    rest = pl.ds(ROWS, (CHUNKS - 1) * ROWS)
    arrived(sib.at[rest], swap_send.at[0], swap_recv.at[0], sibling)
    for j in range(1, CHUNKS):
        merge(j)
        s0(j)
    for j in range(CHUNKS):
        s1(j)
        if j == 4:
            x_step(1)
    s2(0)
    s2(1)
    x_step(2)

    for i in range(CHUNKS):
        s3(i)
        if i + 2 < CHUNKS:
            s2(i + 2)
        if i == 0:
            x_step(3)
        if i == 7:
            reduce_xy(0)
        if i >= 1:
            s4(i - 1)
        if i == 1:
            x_step(4)
            turn_first()
            lax.fori_loop(2, IMAGES, turn, 0)
            send(xt.at[2 * CHUNKS - 1 - core], xt_twin, twin_send.at[0], twin_recv.at[0], sibling)
        if i >= 2:
            shared(i - 2)
            compute(i - 2)
        if i == 6:
            reduce_zc(0)
        flush()
    shared(6)
    compute(6)
    s4(7)
    compute_last()
    reduce_zc(1)
    shared(7)
    tile_last()
    reduced(0)
    accumulate(0, 4)
    reduce_xy(1)
    accumulate(4, 6)
    for copy in sends:
        if copy is not None:
            copy.wait_send()
    reduced(1)
    finish(10, 6)


def shards(patches, out_grads):
    g = out_grads.reshape(CHUNKS * ROWS, COLS)
    bf16 = jnp.bfloat16
    dma = pltpu.SemaphoreType.DMA
    nb = len(BATCHES)
    clipped, norms = pl.pallas_call(
        kernel,
        out_shape=(
            jax.ShapeDtypeStruct((WIDTH, COLS), F32),
            jax.ShapeDtypeStruct((IMAGES, 128), F32),
        ),
        in_specs=[pl.BlockSpec(memory_space=pltpu.HBM)] * 2,
        out_specs=(pl.BlockSpec(memory_space=pltpu.VMEM), pl.BlockSpec(memory_space=pltpu.VMEM)),
        scratch_shapes=[
            pltpu.VMEM((IMAGES, 4, 4, ROWS, COLS), bf16),
            pltpu.VMEM((CHUNKS * ROWS, COLS), bf16),
            pltpu.VMEM((CHUNKS * ROWS, COLS), bf16),
            pltpu.VMEM((8, IMAGES, 32, WIDTH), bf16),
            pltpu.VMEM((IMAGES, WIDTH, SEQ), bf16),
            pltpu.VMEM((2, WIDTH, 2 * SEQ), bf16),
            pltpu.VMEM((WIDTH, SEQ), bf16),
            pltpu.VMEM((2 * len(BATCHES[-1]), WIDTH, COLS), F32),
            pltpu.VMEM((IMAGES, TILE), F32),
            pltpu.VMEM((nb, 16, 16, 128), F32),
            pltpu.VMEM((nb, 16, 16, 128), F32),
            dma((3,)),
            dma((1,)), dma((1,)),
            dma((2, 4)), dma((2, 4)),
            dma((CHUNKS, 16)), dma((CHUNKS, 16)),
            dma((CHUNKS, 8)), dma((CHUNKS, 8)),
            dma((nb, 15)), dma((nb, 16)),
            dma((nb, 15)), dma((nb, 16)),
            dma((1,)), dma((1,)),
        ],
        compiler_params=pltpu.CompilerParams(
            collective_id=0, has_side_effects=True, vmem_limit_bytes=46 * 1024 * 1024
        ),
    )(patches, g)
    return (clipped, norms[:, 0])


def solution(mesh):
    in_specs = (P(None, "col", "row"), P(None, "row", "col"))
    out_specs = (P("row", "col"), P())
    return jax.shard_map(shards, mesh=mesh, in_specs=in_specs, out_specs=out_specs, check_vma=False)
```

```python
import itertools
import math

import jax
import jax.numpy as jnp
from jax import lax
from jax.experimental import pallas as pl
from jax.experimental.pallas import tpu as pltpu
from jax.sharding import PartitionSpec as P

D = 6144
HID = 24576
IMAGES = 16
SEQ = 256
CHUNKS = 8
COARSE = 6
ROWS = 16
WIDTH = 192
COLS = 3072
HALF = COLS // 2
QUARTER = HALF // 2
TILE = 256
BATCHES = ((0, 1, 2, 3, 4), (5, 6, 7))
F32 = jnp.float32


def kernel(
    x_ref, g_ref, out_ref, norms_ref,
    gbuf, own, sib, xbuf, xt, xt_first, xt_twin, tiles, scale, sum_zc, sum_xy,
    local_sem, swap_send, swap_recv, x_send, x_recv,
    ici_send, ici_recv, sib_send, sib_recv,
    zc_send, zc_recv, xy_send, xy_recv, twin_send, twin_recv,
):
    row, z = lax.axis_index("row"), lax.axis_index("col")
    core, y, x = lax.rem(row, 2), lax.rem(row // 2, 4), row // 8

    def at(px, py, pc):
        return {"row": (px * 4 + py) * 2 + pc}

    def up(v, d, n=4):
        return lax.rem(v + d + n, n)

    sibling = at(x, y, 1 - core)
    along_zc = [
        (up(z, dz, 8), lax.rem(core + dc, 2))
        for dz, dc in sorted(itertools.product(range(8), range(2)), key=lambda d: -min(d[0], 8 - d[0]) - d[1])
        if dz or dc
    ]
    along_xy = [
        (up(x, dx), up(y, dy))
        for dx, dy in sorted(itertools.product(range(4), range(4)), key=lambda d: -min(d[0], 4 - d[0]) - min(d[1], 4 - d[1]))
        if dx or dy
    ]
    ahead = [at(up(x, 1), y, core), at(up(x, -1), y, core), at(x, up(y, 1), core), at(x, up(y, -1), core)]

    load_g = pltpu.make_async_copy(g_ref, own, local_sem.at[0])
    load_x = pltpu.make_async_copy(x_ref, xbuf.at[z], local_sem.at[1])
    load_first = pltpu.make_async_copy(g_ref.at[pl.ds(0, ROWS)], gbuf.at[core, x, y], local_sem.at[2])
    load_g.start()
    load_x.start()
    load_first.start()

    barrier = pltpu.get_barrier_semaphore()
    peers = ahead + [{"col": up(z, 1, 8)}, {"col": up(z, -1, 8)}, sibling]
    for peer in peers:
        pl.semaphore_signal(barrier, inc=1, device_id=peer)
    pl.semaphore_wait(barrier, len(peers))

    sends = []

    def send(src, dst, s, r, to, keep=True):
        copy = pltpu.make_async_remote_copy(src, dst, s, r, device_id=to)
        copy.start()
        if keep:
            sends.append(copy)

    def arrived(block, s, r, to):
        pltpu.make_async_remote_copy(block, block, s, r, device_id=to).wait_recv()

    def swap():
        rows = pl.ds(ROWS, (CHUNKS - 1) * ROWS)
        send(g_ref.at[rows], sib.at[rows], swap_send.at[0], swap_recv.at[0], sibling)

    def x_step(s):
        for way, last in ((0, 4), (1, 3)):
            sign = 1 if way == 0 else -1
            if 0 < s <= last:
                block = xbuf.at[up(z, -sign * s, 8)]
                arrived(block, x_send.at[way, s - 1], x_recv.at[way, s - 1], {"col": up(z, sign, 8)})
            if s < last:
                here = up(z, -sign * s, 8)
                src = x_ref if s == 0 else xbuf.at[here]
                send(src, xbuf.at[here], x_send.at[way, s], x_recv.at[way, s], {"col": up(z, sign, 8)})

    def merge(j):
        rows = pl.ds(j * ROWS, ROWS)
        for c in range(0, COLS, 768):
            cols = pl.ds(c, 768)
            a = own[rows, cols].astype(F32)
            b = sib[rows, cols].astype(F32)
            first = jnp.where(core == 0, a[:8], b[8:])
            second = jnp.where(core == 0, b[:8], a[8:])
            both = jnp.concatenate([first, second], axis=0).astype(jnp.bfloat16)
            gbuf[2 * j + core, x, y, :, cols] = both

    def part(b, half, px, py, piece=None):
        start, size = half * HALF, HALF
        if piece is not None:
            start, size = start + piece * QUARTER, QUARTER
        return gbuf.at[b, px, py, :, pl.ds(start, size)]

    everything = slice(None)

    def block(j, half, stage, way, behind):
        b = 2 * j + core
        sign = 1 if way % 2 == 0 else -1
        piece = None if stage % 2 == 0 else way % 2
        if way < 2:
            px, py = up(x, -sign * behind), y
        else:
            px, py = x, up(y, -sign * behind)
        if stage >= 2:
            if half == 0:
                px = everything
            else:
                py = everything
        return part(b, half, px, py, piece)

    def routes(stage):
        for half in range(2):
            along = half if stage < 2 else 1 - half
            for way in (2 * along, 2 * along + 1):
                yield half, way

    def put(j, stage):
        for half, way in routes(stage):
            src = dst = block(j, half, stage, way, stage % 2)
            if j == 0 and stage == 0:
                src = g_ref.at[pl.ds(0, ROWS), pl.ds(half * HALF, HALF)]
            slot = stage * 4 + way
            send(src, dst, ici_send.at[j, slot], ici_recv.at[j, slot], ahead[way])

    def take(j, stage):
        for half, way in routes(stage):
            slot = stage * 4 + way
            arrived(block(j, half, stage, way, 1 + stage % 2), ici_send.at[j, slot], ici_recv.at[j, slot], ahead[way])

    def strip(b, half, d):
        if half == 0:
            return part(b, 0, everything, up(y, d))
        return part(b, 1, up(x, d), everything)

    def share(j, ds):
        if j < COARSE:
            if 2 in ds:
                src = gbuf.at[2 * j + core]
                send(src, src, sib_send.at[j, 0], sib_recv.at[j, 0], sibling)
            return
        for half in range(2):
            for d in ds:
                slot = half * 4 + d
                src = strip(2 * j + core, half, d)
                send(src, src, sib_send.at[j, slot], sib_recv.at[j, slot], sibling)

    def shared(j):
        if j < COARSE:
            arrived(gbuf.at[2 * j + 1 - core], sib_send.at[j, 0], sib_recv.at[j, 0], sibling)
            return
        for half in range(2):
            for d in range(4):
                slot = half * 4 + d
                arrived(strip(2 * j + 1 - core, half, d), sib_send.at[j, slot], sib_recv.at[j, slot], sibling)

    def s0(j):
        put(j, 0)

    def s1(j):
        take(j, 0)
        put(j, 1)

    def s2(j):
        take(j, 1)
        put(j, 2)
        share(j, (0,))

    def s3(j):
        take(j, 2)
        put(j, 3)
        share(j, (1, 3))

    def s4(j):
        take(j, 3)
        share(j, (2,))

    def turn(b, carry):
        xt[b] = xbuf[:, b].reshape(SEQ, WIDTH).astype(F32).T.astype(jnp.bfloat16)
        return carry

    def turn_first():
        for b in range(2):
            halves = xbuf[:, b].reshape(ROWS, 2, 8, WIDTH).astype(F32)
            nothing = jnp.zeros((ROWS, 8, WIDTH), F32)
            for h in range(2):
                pair = [halves[:, h], nothing] if b == 0 else [nothing, halves[:, h]]
                rows = jnp.stack(pair, axis=1).reshape(SEQ, WIDTH)
                xt_first[b, :, h * SEQ : (h + 1) * SEQ] = rows.T.astype(jnp.bfloat16)

    def product(b, cols):
        if isinstance(b, int) and b < 2:
            g = gbuf[0:2, :, :, :, cols].reshape(2 * SEQ, TILE)
            return jnp.dot(xt_first[b], g, preferred_element_type=F32)
        g = gbuf[b, :, :, :, cols].reshape(SEQ, TILE)
        return jnp.dot(xt[b], g, preferred_element_type=F32)

    def squares(b, slot):
        acc = jnp.zeros((8, 128), F32)
        for n in range(0, COLS, TILE):
            cols = pl.ds(n, TILE)
            t = product(b, cols)
            if slot is not None:
                tiles[slot, :, cols] = t
            s = (t * t).reshape(WIDTH // 8, 8, TILE).sum(axis=0)
            acc = acc + s[:, :128] + s[:, 128:]
        return jnp.sum(acc, axis=0, keepdims=True)

    def images(k):
        return [b for j in BATCHES[k] for b in (2 * j, 2 * j + 1)]

    def compute(j):
        k = [i for i, batch in enumerate(BATCHES) if j in batch][0]
        first, last = images(k)[0], k == len(BATCHES) - 1
        me = z * 2 + core

        def one(b, carry):
            sum_zc[k, me, pl.ds(b - first, 1), :] = squares(b, b - first if last else None)
            return carry

        if j == 0:
            one(0, 0)
            one(1, 0)
        else:
            lax.fori_loop(2 * j, 2 * j + 2, one, 0)

    def compute_last():
        b = 2 * (CHUNKS - 1) + core
        arrived(xt_twin, twin_send.at[0], twin_recv.at[0], sibling)
        acc = jnp.zeros((8, 128), F32)
        for n in range(0, COLS, TILE):
            cols = pl.ds(n, TILE)
            g = gbuf[b, :, :, :, cols].reshape(SEQ, TILE)
            mine = jnp.dot(xt[b], g, preferred_element_type=F32)
            twin = jnp.dot(xt_twin[...], g, preferred_element_type=F32)
            tiles[4 + core, :, cols] = mine
            s = (mine * mine + twin * twin).reshape(WIDTH // 8, 8, TILE).sum(axis=0)
            acc = acc + s[:, :128] + s[:, 128:]
        sum_zc[1, z * 2 + core, pl.ds(4 + core, 1), :] = jnp.sum(acc, axis=0, keepdims=True)

    def tile_last():
        b = 2 * CHUNKS - 1 - core
        for n in range(0, COLS, TILE):
            cols = pl.ds(n, TILE)
            tiles[5 - core, :, cols] = product(b, cols)

    def rows_of(k):
        return 8 if len(images(k)) <= 8 else 16

    def reduce_zc(k):
        me = z * 2 + core
        rows = pl.ds(0, rows_of(k))
        mine = sum_zc.at[k, me, rows]
        for i, (pz, pc) in enumerate(along_zc):
            send(mine, mine, zc_send.at[k, i], zc_recv.at[k, me], dict(at(x, y, pc), col=pz))

    def reduce_xy(k):
        rows = pl.ds(0, rows_of(k))
        for i, (pz, pc) in enumerate(along_zc):
            it = pz * 2 + pc
            arrived(sum_zc.at[k, it, rows], zc_send.at[k, i], zc_recv.at[k, it], dict(at(x, y, pc), col=pz))
        me = x * 4 + y
        sum_xy[k, me, rows] = jnp.sum(sum_zc[k, :, rows], axis=0)
        mine = sum_xy.at[k, me, rows]
        for i, (px, py) in enumerate(along_xy):
            send(mine, mine, xy_send.at[k, i], xy_recv.at[k, me], at(px, py, core))

    def reduced(k):
        rows = pl.ds(0, rows_of(k))
        for i, (px, py) in enumerate(along_xy):
            it = px * 4 + py
            arrived(sum_xy.at[k, it, rows], xy_send.at[k, i], xy_recv.at[k, it], at(px, py, core))
        total = jnp.sum(jnp.sum(sum_xy[k, :, rows], axis=0), axis=1, keepdims=True)
        norm = jnp.sqrt(total) / math.sqrt(D * HID)
        norm = jnp.broadcast_to(norm, (rows_of(k), TILE))
        first, count = images(k)[0], len(images(k))
        norms_ref[first : first + count, :] = norm[:count, :128]
        scale[first : first + count, :] = (1.0 / jnp.maximum(norm, 1.0))[:count]

    def accumulate(first, count):
        def add(b):
            for n in range(0, COLS, TILE):
                cols = pl.ds(n, TILE)
                acc = scale[pl.ds(b, 1), :] * product(b, cols) + scale[pl.ds(b + 1, 1), :] * product(b + 1, cols)
                out_ref[:, cols] = acc if isinstance(b, int) and b == 0 else out_ref[:, cols] + acc

        def pair(i, carry):
            add(first + 2 * i)
            return carry

        if first == 0:
            add(0)
        lax.fori_loop(1 if first == 0 else 0, count // 2, pair, 0)

    def finish(first, count):
        for n in range(0, COLS, TILE):
            cols = pl.ds(n, TILE)
            acc = out_ref[:, cols]
            for i in range(count):
                acc = acc + scale[first + i : first + i + 1, :] * tiles[i, :, cols]
            out_ref[:, cols] = acc

    marks = [0]

    def flush():
        for copy in sends[: marks[-2] if len(marks) > 1 else 0]:
            if copy is not None:
                copy.wait_send()
        for i in range(marks[-2] if len(marks) > 1 else 0):
            sends[i] = None
        marks.append(len(sends))

    s0(0)
    swap()
    x_step(0)
    for k in range(len(BATCHES)):
        sum_zc[k, z * 2 + core] = jnp.zeros((16, 128), F32)
    load_g.wait()
    load_x.wait()
    load_first.wait()
    rest = pl.ds(ROWS, (CHUNKS - 1) * ROWS)
    arrived(sib.at[rest], swap_send.at[0], swap_recv.at[0], sibling)
    for j in range(1, CHUNKS):
        merge(j)
        s0(j)
    for j in range(CHUNKS):
        s1(j)
        if j == 4:
            x_step(1)
    s2(0)
    s2(1)
    x_step(2)

    for i in range(CHUNKS):
        s3(i)
        if i + 2 < CHUNKS:
            s2(i + 2)
        if i == 1:
            x_step(3)
        if i == 7:
            reduce_xy(0)
        if i >= 1:
            s4(i - 1)
        if i == 2:
            x_step(4)
            turn_first()
            lax.fori_loop(2, IMAGES, turn, 0)
            send(xt.at[2 * CHUNKS - 1 - core], xt_twin, twin_send.at[0], twin_recv.at[0], sibling)
        if i >= 2:
            shared(i - 2)
            compute(i - 2)
        if i == 6:
            reduce_zc(0)
        flush()
    shared(6)
    compute(6)
    s4(7)
    compute_last()
    reduce_zc(1)
    shared(7)
    tile_last()
    reduced(0)
    accumulate(0, 4)
    reduce_xy(1)
    accumulate(4, 6)
    for copy in sends:
        if copy is not None:
            copy.wait_send()
    reduced(1)
    finish(10, 6)


def shards(patches, out_grads):
    g = out_grads.reshape(CHUNKS * ROWS, COLS)
    bf16 = jnp.bfloat16
    dma = pltpu.SemaphoreType.DMA
    nb = len(BATCHES)
    clipped, norms = pl.pallas_call(
        kernel,
        out_shape=(
            jax.ShapeDtypeStruct((WIDTH, COLS), F32),
            jax.ShapeDtypeStruct((IMAGES, 128), F32),
        ),
        in_specs=[pl.BlockSpec(memory_space=pltpu.HBM)] * 2,
        out_specs=(pl.BlockSpec(memory_space=pltpu.VMEM), pl.BlockSpec(memory_space=pltpu.VMEM)),
        scratch_shapes=[
            pltpu.VMEM((IMAGES, 4, 4, ROWS, COLS), bf16),
            pltpu.VMEM((CHUNKS * ROWS, COLS), bf16),
            pltpu.VMEM((CHUNKS * ROWS, COLS), bf16),
            pltpu.VMEM((8, IMAGES, 32, WIDTH), bf16),
            pltpu.VMEM((IMAGES, WIDTH, SEQ), bf16),
            pltpu.VMEM((2, WIDTH, 2 * SEQ), bf16),
            pltpu.VMEM((WIDTH, SEQ), bf16),
            pltpu.VMEM((2 * len(BATCHES[-1]), WIDTH, COLS), F32),
            pltpu.VMEM((IMAGES, TILE), F32),
            pltpu.VMEM((nb, 16, 16, 128), F32),
            pltpu.VMEM((nb, 16, 16, 128), F32),
            dma((3,)),
            dma((1,)), dma((1,)),
            dma((2, 4)), dma((2, 4)),
            dma((CHUNKS, 16)), dma((CHUNKS, 16)),
            dma((CHUNKS, 8)), dma((CHUNKS, 8)),
            dma((nb, 15)), dma((nb, 16)),
            dma((nb, 15)), dma((nb, 16)),
            dma((1,)), dma((1,)),
        ],
        compiler_params=pltpu.CompilerParams(
            collective_id=0, has_side_effects=True, vmem_limit_bytes=46 * 1024 * 1024
        ),
    )(patches, g)
    return (clipped, norms[:, 0])


def solution(mesh):
    in_specs = (P(None, "col", "row"), P(None, "row", "col"))
    out_specs = (P("row", "col"), P())
    return jax.shard_map(shards, mesh=mesh, in_specs=in_specs, out_specs=out_specs, check_vma=False)
```
